32 devices in a mesh: ctx: 16 (over z, y, core), fsdp: 2 (over x).
Axes of the slice: x: 2, y: 2, z: 4, core: 2. Of those that a mesh axis runs over, the one named last changes fastest.
Arguments:
- tokens: bfloat16 [2, 2048, 960], P('fsdp', 'ctx'), may hold values from -6 to 6
- pair_of: int32 [2, 16], P('fsdp'), may hold values from 0 to 15, each once within a row
- attn_gain: bfloat16 [960], P('fsdp'), may hold values from 0.25 to 1.75
- w_query: bfloat16 [960, 960], P('fsdp'), may hold values from -0.1875 to 0.1875
- w_key: bfloat16 [960, 320], P('fsdp'), may hold values from -0.1875 to 0.1875
- w_value: bfloat16 [960, 320], P('fsdp'), may hold values from -0.1875 to 0.1875
- w_out: bfloat16 [960, 960], P('fsdp'), may hold values from -0.75 to 0.75
- ffn_gain: bfloat16 [960], P('fsdp'), may hold values from 0.25 to 1.75
- w_gate: bfloat16 [960, 2560], P('fsdp'), may hold values from -0.1875 to 0.1875
- w_up: bfloat16 [960, 2560], P('fsdp'), may hold values from -0.1875 to 0.1875
- w_down: bfloat16 [2560, 960], P('fsdp'), may hold values from -0.125 to 0.125
- out_grad: bfloat16 [2, 2048, 960], P('fsdp', 'ctx'), may hold values from -6 to 6
Outputs:
- block_out: bfloat16 [2, 2048, 960], P('fsdp', 'ctx')
- grad_in: float32 [2, 2048, 960], P('fsdp', 'ctx')
- grad_attn_gain: float32 [960], P('fsdp')
- grad_query: float32 [960, 960], P('fsdp')
- grad_key: float32 [960, 320], P('fsdp')
- grad_value: float32 [960, 320], P('fsdp')
- grad_out_proj: float32 [960, 960], P('fsdp')
- grad_ffn_gain: float32 [960], P('fsdp')
- grad_gate: float32 [960, 2560], P('fsdp')
- grad_up: float32 [960, 2560], P('fsdp')
- grad_down: float32 [2560, 960], P('fsdp')
The draws below stay inside these ranges and needn't reach their ends.
Inputs may be any that keep to these rules, and one draw needn't show every extreme that they name: `pair_of`: each row names every number below 16 once.
All inputs are finite; a program needn't handle non-finite values.
Results may differ from the reference program's by a relative error of at most 0.024.
Values may be sent and summed in bfloat16 or wider, within the bound.
A program may use at most 192 MiB of HBM per device.

```python
import math
import jax
import jax.numpy as jnp
from jax import lax

D = 960
HEADS = 15
KV_HEADS = 5
HEAD = 64
FF = 2560
TOK_DEV = 128
SEQS = 2
PAIRS = 16
SEQ_LEN = 2048


def steps_of(rng, shape, cuts, low, largest):
    gain, own = 1.0, jax.random.fold_in(rng, 6)
    for position, parts in cuts:
        heights = jnp.exp(jax.random.uniform(jax.random.fold_in(own, position), (parts,), jnp.float32, low / len(cuts), largest / len(cuts)))
        gain = gain * jnp.repeat(heights, shape[position] // parts).reshape([-1 if axis == position else 1 for axis in range(len(shape))])
    return gain


def gaussian(rng, shape, spread, bound, split=(), kind=jnp.bfloat16):
    values = jax.random.normal(rng, shape, jnp.float32) * spread
    if len(split) > 0:
        values = steps_of(rng, shape, split, -0.22, 0.18) * values
    return jnp.clip(values, min=-bound, max=bound).astype(kind)


def setup_inputs(seed: int = 0) -> dict:
    key_of = jax.random.split(jax.random.key(seed), 13)
    return {
        "tokens": gaussian(key_of[0], (SEQS, SEQ_LEN, D), 1.0, 6.0, ((0, 2), (1, 16))),
        "pair_of": jax.vmap(lambda own: jax.random.permutation(own, PAIRS))(jax.random.split(key_of[1], SEQS)).reshape((SEQS, PAIRS)).astype(jnp.int32),
        "attn_gain": jnp.clip(1.0 + 0.15 * jax.random.normal(key_of[2], (D,), jnp.float32), 0.25, 1.75).astype(jnp.bfloat16),
        "w_query": gaussian(key_of[3], (D, HEADS * HEAD), D ** -0.5, 0.1875, ((0, 2),)),
        "w_key": gaussian(key_of[4], (D, KV_HEADS * HEAD), D ** -0.5, 0.1875, ((0, 2),)),
        "w_value": gaussian(key_of[5], (D, KV_HEADS * HEAD), D ** -0.5, 0.1875, ((0, 2),)),
        "w_out": gaussian(key_of[6], (HEADS * HEAD, D), HEAD ** -0.5, 0.75, ((0, 2),)),
        "ffn_gain": jnp.clip(1.0 + 0.15 * jax.random.normal(key_of[7], (D,), jnp.float32), 0.25, 1.75).astype(jnp.bfloat16),
        "w_gate": gaussian(key_of[8], (D, FF), D ** -0.5, 0.1875, ((0, 2),)),
        "w_up": gaussian(key_of[9], (D, FF), D ** -0.5, 0.1875, ((0, 2),)),
        "w_down": gaussian(key_of[10], (FF, D), FF ** -0.5, 0.125, ((0, 2),)),
        "out_grad": gaussian(key_of[11], (SEQS, SEQ_LEN, D), 1.0, 6.0, ((0, 2), (1, 16))),
    }


NORM_EPS = 1e-05
ROPE_BASE = 100000.0
MASKED = -1e+30

@jax.custom_vjp
def low(v):
    return lax.optimization_barrier(v.astype(jnp.bfloat16)).astype(jnp.float32)

@jax.custom_vjp
def low_back(v):
    return v

def low_keep(v):
    return (low(v), None)

def low_pass(kept, grad):
    return (grad,)

def back_keep(v):
    return (v, None)

def back_low(kept, grad):
    return (low(grad),)
low.defvjp(low_keep, low_pass)
low_back.defvjp(back_keep, back_low)

def dot_high(left_mat, right_mat):
    return jnp.dot(left_mat, right_mat, precision=lax.Precision.HIGHEST, preferred_element_type=jnp.float32)

def rms_scale(source, gain_vec):
    return source * lax.rsqrt(lax.optimization_barrier(jnp.mean(source * source, axis=-1, keepdims=True)) + NORM_EPS) * gain_vec

def rope_tables(positions, head_size):
    half_size = head_size // 2
    exponent = jnp.arange(half_size, dtype=jnp.float32) * (2.0 / head_size)
    frequency = jnp.exp(-exponent * math.log(ROPE_BASE))
    angle_table = positions.astype(jnp.float32)[:, None] * frequency[None, :]
    return (jnp.cos(angle_table)[:, None, :], jnp.sin(angle_table)[:, None, :])

def rotate(vectors, cosine_table, sine_table):
    half_size = vectors.shape[-1] // 2
    front_half = vectors[..., :half_size]
    back_half = vectors[..., half_size:]
    return jnp.concatenate([front_half * cosine_table - back_half * sine_table, back_half * cosine_table + front_half * sine_table], axis=-1)

def token_positions(pair_row):
    pair_total = pair_row.shape[0]
    half_rows = TOK_DEV // 2
    block_ids = jnp.stack([pair_row, 2 * pair_total - 1 - pair_row], axis=1)
    offsets = jnp.arange(half_rows, dtype=jnp.int32)
    return (block_ids[:, :, None] * half_rows + offsets[None, None, :]).reshape(pair_total * TOK_DEV)

def attend(queries, key_rows, value_rows, positions):
    length = queries.shape[0]
    group_size = HEADS // KV_HEADS
    query_block = min(512, length)
    query_blocks = queries.reshape(length // query_block, query_block, KV_HEADS, group_size, HEAD)
    pos_blocks = positions.reshape(length // query_block, query_block)

    def one_block(block_args):
        query_part, pos_part = block_args
        scores = jnp.einsum('qkgd,tkd->kgqt', query_part, key_rows, precision=lax.Precision.HIGHEST) * HEAD ** (-0.5)
        scores = low_back(scores)
        visible = positions[None, None, None, :] <= pos_part[None, None, :, None]
        scores = jnp.where(visible, scores, MASKED)
        row_max = lax.optimization_barrier(jnp.max(scores, axis=-1, keepdims=True))
        expd = jnp.exp(scores - row_max)
        probs = expd / lax.optimization_barrier(jnp.sum(expd, axis=-1, keepdims=True))
        return jnp.einsum('kgqt,tkd->qkgd', low(probs), value_rows, precision=lax.Precision.HIGHEST)
    result = lax.map(jax.checkpoint(one_block), (query_blocks, pos_blocks))
    return result.reshape(length, HEADS * HEAD)

def layer_forward(source, positions, gain_attn, query_w, key_w, value_w, out_w, gain_ffn, gate_w, up_w, down_w):
    length = source.shape[0]
    cosine_table, sine_table = rope_tables(positions, HEAD)
    normed_one = low(rms_scale(source, gain_attn))
    query_raw = low_back(dot_high(normed_one, query_w)).reshape(length, HEADS, HEAD)
    key_raw = low_back(dot_high(normed_one, key_w)).reshape(length, KV_HEADS, HEAD)
    value_rows = low(low_back(dot_high(normed_one, value_w))).reshape(length, KV_HEADS, HEAD)
    queries = low(rotate(query_raw, cosine_table, sine_table))
    key_rows = low(rotate(key_raw, cosine_table, sine_table))
    mixed = low(low_back(attend(queries, key_rows, value_rows, positions)))
    residual = source + low_back(dot_high(mixed, out_w))
    normed_two = low(rms_scale(residual, gain_ffn))
    gate_pre = low_back(dot_high(normed_two, gate_w))
    up_pre = low_back(dot_high(normed_two, up_w))
    hidden = low(gate_pre * jax.nn.sigmoid(gate_pre) * up_pre)
    return residual + low_back(dot_high(hidden, down_w))

def reference(tokens, pair_of, attn_gain, w_query, w_key, w_value, w_out, ffn_gain, w_gate, w_up, w_down, out_grad):
    params = tuple((weight.astype(jnp.float32) for weight in (attn_gain, w_query, w_key, w_value, w_out, ffn_gain, w_gate, w_up, w_down)))

    def per_sequence(totals, sequence):
        seq_tokens, seq_cotangent, pair_row = sequence
        positions = token_positions(pair_row)

        def forward_of(source, *weight_list):
            return layer_forward(source, positions, *weight_list)
        result, pullback = jax.vjp(forward_of, seq_tokens.astype(jnp.float32), *params)
        gradients = pullback(seq_cotangent.astype(jnp.float32))
        totals = tuple((running + extra for running, extra in zip(totals, gradients[1:])))
        return (totals, (result.astype(jnp.bfloat16), gradients[0]))
    initial = tuple((jnp.zeros(weight.shape, jnp.float32) for weight in params))
    totals, outputs = lax.scan(per_sequence, initial, (tokens, out_grad, pair_of))
    return (outputs[0], outputs[1], totals[0], totals[1], totals[2], totals[3], totals[4], totals[5], totals[6], totals[7], totals[8])
```

```python
import math

import jax
import jax.numpy as jnp
from jax import lax
from jax.sharding import PartitionSpec as P

HEADS = 15
KV_HEADS = 5
HEAD = 64


NORM_EPS = 1e-05
ROPE_BASE = 100000.0
MASKED = -1e30
TILE_KEYS = 512


def matmul(left_mat, right_mat):
    return jnp.dot(left_mat, right_mat, preferred_element_type=jnp.float32)


def contract_rows(left_mat, right_mat):
    return lax.dot_general(
        left_mat, right_mat, (((0,), (0,)), ((), ())), preferred_element_type=jnp.float32
    )


def contract_cols(left_mat, right_mat):
    return lax.dot_general(
        left_mat, right_mat, (((1,), (1,)), ((), ())), preferred_element_type=jnp.float32
    )


def rope_tables(positions, head_size):
    half_size = head_size // 2
    exponent = jnp.arange(half_size, dtype=jnp.float32) * (2.0 / head_size)
    frequency = jnp.exp(-exponent * math.log(ROPE_BASE))
    angle_table = positions.astype(jnp.float32)[:, None] * frequency[None, :]
    return (jnp.cos(angle_table)[:, None, :], jnp.sin(angle_table)[:, None, :])


def rotate(vectors, cosine_table, sine_table):
    half_size = vectors.shape[-1] // 2
    front_half = vectors[..., :half_size]
    back_half = vectors[..., half_size:]
    return jnp.concatenate(
        [
            front_half * cosine_table - back_half * sine_table,
            back_half * cosine_table + front_half * sine_table,
        ],
        axis=-1,
    )


def unrotate(grad_vec, cosine_table, sine_table):
    half_size = grad_vec.shape[-1] // 2
    front_half = grad_vec[..., :half_size]
    back_half = grad_vec[..., half_size:]
    return jnp.concatenate(
        [
            front_half * cosine_table + back_half * sine_table,
            back_half * cosine_table - front_half * sine_table,
        ],
        axis=-1,
    )


def inverse_rms(source):
    return lax.rsqrt(jnp.mean(source * source, axis=-1, keepdims=True) + NORM_EPS)


def norm_back(grad_normed, source, inverse, gain_vec):
    scaled = grad_normed * gain_vec
    inner = jnp.sum(scaled * source, axis=-1, keepdims=True) / source.shape[-1]
    grad_source = inverse * scaled - source * (inverse * inverse * inverse) * inner
    grad_gain = jnp.sum(grad_normed * source * inverse, axis=0)
    return (grad_source, grad_gain)


def reorder_blocks(rows_in, block_order, block_rows):
    blocks = rows_in.reshape((block_order.shape[0], block_rows) + rows_in.shape[1:])
    return jnp.take(blocks, block_order, axis=0).reshape(rows_in.shape)


def tile_scores(queries, key_tile, query_pos, first_key, score_scale):
    key_span = key_tile.shape[0]
    scores = (
        jnp.einsum("qkgd,tkd->kgqt", queries, key_tile, preferred_element_type=jnp.float32)
        * score_scale
    )
    key_pos = first_key + jnp.arange(key_span, dtype=jnp.int32)
    visible = key_pos[None, None, None, :] <= query_pos[None, None, :, None]
    return jnp.where(visible, scores, MASKED)


def block_forward(
    queries, query_pos, keys_natural, values_natural, tile_count, key_span, score_scale
):
    stat_shape = (queries.shape[1], queries.shape[2], queries.shape[0])

    def stats_step(tile_index, running):
        row_max, row_sum = running
        key_tile = lax.dynamic_slice_in_dim(keys_natural, tile_index * key_span, key_span, 0)
        scores = tile_scores(queries, key_tile, query_pos, tile_index * key_span, score_scale)
        new_max = jnp.maximum(row_max, jnp.max(scores, axis=-1))
        row_sum = row_sum * jnp.exp(row_max - new_max) + jnp.sum(
            jnp.exp(scores - new_max[..., None]), axis=-1
        )
        return (new_max, row_sum)

    initial = (jnp.full(stat_shape, MASKED, jnp.float32), jnp.zeros(stat_shape, jnp.float32))
    row_max, row_sum = lax.fori_loop(0, tile_count, stats_step, initial)

    def value_step(tile_index, accumulated):
        key_tile = lax.dynamic_slice_in_dim(keys_natural, tile_index * key_span, key_span, 0)
        value_tile = lax.dynamic_slice_in_dim(values_natural, tile_index * key_span, key_span, 0)
        scores = tile_scores(queries, key_tile, query_pos, tile_index * key_span, score_scale)
        weights = (jnp.exp(scores - row_max[..., None]) / row_sum[..., None]).astype(jnp.bfloat16)
        return accumulated + jnp.einsum(
            "kgqt,tkd->qkgd", weights, value_tile, preferred_element_type=jnp.float32
        )

    mixed_part = lax.fori_loop(0, tile_count, value_step, jnp.zeros(queries.shape, jnp.float32))
    return (mixed_part, row_max, row_sum)


def block_backward(
    queries,
    query_pos,
    keys_natural,
    values_natural,
    tile_count,
    key_span,
    score_scale,
    row_max,
    row_sum,
    grad_mixed,
    row_delta,
    grad_keys,
    grad_values,
):

    def grad_step(tile_index, running):
        grad_query, key_buffer, value_buffer = running
        first_key = tile_index * key_span
        key_tile = lax.dynamic_slice_in_dim(keys_natural, first_key, key_span, 0)
        value_tile = lax.dynamic_slice_in_dim(values_natural, first_key, key_span, 0)
        scores = tile_scores(queries, key_tile, query_pos, first_key, score_scale)
        probs = jnp.exp(scores - row_max[..., None]) / row_sum[..., None]
        probs_low = probs.astype(jnp.bfloat16)
        grad_probs = jnp.einsum(
            "qkgd,tkd->kgqt", grad_mixed, value_tile, preferred_element_type=jnp.float32
        )
        grad_scores = (probs * (grad_probs - row_delta[..., None])).astype(jnp.bfloat16)
        grad_query = grad_query + jnp.einsum(
            "kgqt,tkd->qkgd", grad_scores, key_tile, preferred_element_type=jnp.float32
        )
        key_part = jnp.einsum(
            "kgqt,qkgd->tkd", grad_scores, queries, preferred_element_type=jnp.float32
        )
        value_part = jnp.einsum(
            "kgqt,qkgd->tkd", probs_low, grad_mixed, preferred_element_type=jnp.float32
        )
        key_buffer = lax.dynamic_update_slice_in_dim(
            key_buffer,
            lax.dynamic_slice_in_dim(key_buffer, first_key, key_span, 0) + key_part,
            first_key,
            0,
        )
        value_buffer = lax.dynamic_update_slice_in_dim(
            value_buffer,
            lax.dynamic_slice_in_dim(value_buffer, first_key, key_span, 0) + value_part,
            first_key,
            0,
        )
        return (grad_query, key_buffer, value_buffer)

    initial = (jnp.zeros(queries.shape, jnp.float32), grad_keys, grad_values)
    return lax.fori_loop(0, tile_count, grad_step, initial)


def bit_of(axis_name, bit):
    return (lax.axis_index(axis_name) >> bit) & 1


def swap(array, axis_name, bit):
    size = lax.axis_size(axis_name)
    return lax.ppermute(array, axis_name, [(i, i ^ (1 << bit)) for i in range(size)])


def bits_of(axis_name):
    return lax.axis_size(axis_name).bit_length() - 1


def half_of(array, index, dim):
    size = array.shape[dim] // 2
    return lax.dynamic_slice_in_dim(array, index * size, size, dim)


def join(mine, other, bit, dim):
    first = jnp.where(bit == 0, mine, other)
    second = jnp.where(bit == 0, other, mine)
    return jnp.concatenate([first, second], axis=dim)


def gather_weight(shard):
    core = bit_of("ctx", 0)
    part = half_of(shard, core, 0)[None]
    size = lax.axis_size("fsdp")
    pieces = [
        lax.ppermute(part, "fsdp", [(i, (i + step) % size) for i in range(size)])
        for step in range(1, size)
    ]
    pieces = [join(piece, swap(piece, "ctx", 0), core, 1) for piece in pieces]
    own = lax.axis_index("fsdp")
    rows = shard.shape[0]
    if size == 2:
        return join(shard, pieces[0][0], own, 0)
    full = jnp.zeros((size * rows,) + shard.shape[1:], shard.dtype)
    full = lax.dynamic_update_slice_in_dim(full, shard, own * rows, 0)
    for step, piece in enumerate(pieces):
        source = (own - step - 1 + size) % size
        full = lax.dynamic_update_slice_in_dim(full, piece[0], source * rows, 0)
    return full


def split_dim(shape):
    rows, columns = shape[1], shape[2]
    if rows % 16 == 0:
        return 1
    if columns % 256 == 0 or rows % 2:
        return 2
    return 1 if columns % 2 else 2


def reduce_owner(parts, order):
    trail = []
    held = parts
    for axis_name, bit in order:
        dim = 0 if axis_name == "fsdp" else split_dim(held.shape)
        own = bit_of(axis_name, bit)
        other = swap(half_of(held, 1 - own, dim), axis_name, bit)
        kept = half_of(held, own, dim)
        held = (kept.astype(jnp.float32) + other.astype(jnp.float32)).astype(jnp.bfloat16)
        if axis_name == "ctx":
            trail.append((bit, dim))
    return held, trail


def spread_owner(held, trail):
    for bit, dim in reversed(trail):
        held = join(held, swap(held, "ctx", bit), bit_of("ctx", bit), dim)
    return held


def orders():
    fsdp = [("fsdp", bit) for bit in reversed(range(bits_of("fsdp")))]
    ctx = [("ctx", bit) for bit in range(1, bits_of("ctx"))]
    return fsdp, ctx


def body(
    tokens,
    pair_of,
    attn_gain,
    w_query,
    w_key,
    w_value,
    w_out,
    ffn_gain,
    w_gate,
    w_up,
    w_down,
    out_grad,
):
    inputs = tokens[0].astype(jnp.float32)
    local_rows = inputs.shape[0]
    half_rows = local_rows // 2
    pair_row = pair_of[0]
    pair_total = lax.axis_size("ctx")
    seq_length = pair_total * local_rows
    key_span = min(TILE_KEYS, seq_length)
    score_scale = HEAD ** (-0.5)
    group_size = HEADS // KV_HEADS
    first_bundle = jnp.concatenate(
        [w_query, w_key, w_value, attn_gain[:, None], ffn_gain[:, None]], axis=1
    )
    first_full = gather_weight(first_bundle)
    kv_size = KV_HEADS * HEAD
    q_size = HEADS * HEAD
    qkv_size = q_size + 2 * kv_size
    qkv_full = first_full[:, :qkv_size]
    gain_attn = first_full[:, qkv_size]
    gain_ffn = first_full[:, qkv_size + 1]
    w_out, w_gate, w_up, w_down, first_full = lax.optimization_barrier(
        (w_out, w_gate, w_up, w_down, first_full)
    )
    out_full = gather_weight(w_out)
    gate_full = gather_weight(w_gate)
    up_full = gather_weight(w_up)
    down_full = gather_weight(w_down)
    gain_attn = gain_attn.astype(jnp.float32)
    gain_ffn = gain_ffn.astype(jnp.float32)
    slot_ids = jnp.arange(pair_total, dtype=jnp.int32)
    own_pair = jnp.sum(jnp.where(slot_ids == lax.axis_index("ctx"), pair_row, 0))
    own_blocks = jnp.stack([own_pair, 2 * pair_total - 1 - own_pair])
    offsets = jnp.arange(half_rows, dtype=jnp.int32)
    own_pos = (own_blocks[:, None] * half_rows + offsets[None, :]).reshape(local_rows)
    cosine_table, sine_table = rope_tables(own_pos, HEAD)
    holder = jnp.sum(
        jnp.where(pair_row[None, :] == slot_ids[:, None], slot_ids[None, :], 0), axis=1
    )
    own_slot = lax.axis_index("ctx")
    relative = holder ^ own_slot
    natural_order = jnp.concatenate([relative * 2, (relative * 2 + 1)[::-1]])
    relative_pair = jnp.take(pair_row, slot_ids ^ own_slot)
    device_order = jnp.stack([relative_pair, 2 * pair_total - 1 - relative_pair], axis=1).reshape(
        2 * pair_total
    )
    inverse_one = inverse_rms(inputs)
    normed_one = (inputs * inverse_one * gain_attn).astype(jnp.bfloat16)
    raw_all = matmul(normed_one, qkv_full)
    query_raw = raw_all[:, :q_size].reshape(local_rows, HEADS, HEAD)
    key_raw = raw_all[:, q_size : q_size + kv_size].reshape(local_rows, KV_HEADS, HEAD)
    value_local = raw_all[:, q_size + kv_size :].astype(jnp.bfloat16)
    queries = (
        rotate(query_raw, cosine_table, sine_table)
        .astype(jnp.bfloat16)
        .reshape(local_rows, KV_HEADS, group_size, HEAD)
    )
    key_local = (
        rotate(key_raw, cosine_table, sine_table)
        .astype(jnp.bfloat16)
        .reshape(local_rows, KV_HEADS * HEAD)
    )
    ctx_bits = bits_of("ctx")
    both = jnp.concatenate([key_local, value_local], axis=1)[None]
    for bit in reversed(range(ctx_bits)):
        both = jnp.stack([both, swap(both, "ctx", bit)], axis=1).reshape(
            (2 * both.shape[0],) + both.shape[1:]
        )
    both_natural = reorder_blocks(
        both.reshape(seq_length, 2 * kv_size), natural_order, half_rows
    )
    keys_natural = both_natural[:, :kv_size].reshape(seq_length, KV_HEADS, HEAD)
    values_natural = both_natural[:, kv_size:].reshape(seq_length, KV_HEADS, HEAD)
    tile_counts = (own_blocks * half_rows + half_rows - 1) // key_span + 1
    mixed_parts = []
    stat_parts = []
    for half_index in range(2):
        low_row = half_index * half_rows
        high_row = low_row + half_rows
        mixed_part, row_max, row_sum = block_forward(
            queries[low_row:high_row],
            own_pos[low_row:high_row],
            keys_natural,
            values_natural,
            tile_counts[half_index],
            key_span,
            score_scale,
        )
        mixed_parts.append(mixed_part)
        stat_parts.append((row_max, row_sum))
    mixed_full = jnp.concatenate(mixed_parts, axis=0)
    mixed_low = mixed_full.reshape(local_rows, HEADS * HEAD).astype(jnp.bfloat16)
    residual = inputs + matmul(mixed_low, out_full)
    inverse_two = inverse_rms(residual)
    normed_two = (residual * inverse_two * gain_ffn).astype(jnp.bfloat16)
    columns = normed_two
    gate_pre = matmul(columns, gate_full)
    up_pre = matmul(columns, up_full)
    sigmoid_gate = jax.nn.sigmoid(gate_pre)
    activated = gate_pre * sigmoid_gate
    hidden = (activated * up_pre).astype(jnp.bfloat16)
    columns = hidden
    down_out = matmul(columns, down_full)
    block_out = (residual + down_out).astype(jnp.bfloat16)[None]
    grad_z = out_grad[0]
    grad_hidden = contract_cols(grad_z, down_full)
    grad_gate_low = (
        grad_hidden * up_pre * sigmoid_gate * (1.0 + gate_pre * (1.0 - sigmoid_gate))
    ).astype(jnp.bfloat16)
    grad_up_low = (grad_hidden * activated).astype(jnp.bfloat16)
    part = contract_cols(grad_gate_low, gate_full) + contract_cols(grad_up_low, up_full)
    owners = lax.axis_size("fsdp")
    core = bit_of("ctx", 0)
    fsdp_order, ctx_order = orders()
    core_order = [("ctx", 0)]

    def by_owner(left_mat, right_mat):
        product = contract_rows(left_mat, right_mat).astype(jnp.bfloat16)
        return product.reshape((owners, product.shape[0] // owners, product.shape[1]))

    down_held, down_trail = reduce_owner(
        by_owner(hidden, grad_z), core_order + ctx_order + fsdp_order
    )
    grad_down = spread_owner(down_held, down_trail)[0].astype(jnp.float32)
    gate_up_other = swap(
        by_owner(normed_two, jnp.where(core == 0, grad_up_low, grad_gate_low)), "ctx", 0
    )
    gate_up_mine = by_owner(normed_two, jnp.where(core == 0, grad_gate_low, grad_up_low))
    gate_up = (gate_up_mine.astype(jnp.float32) + gate_up_other.astype(jnp.float32)).astype(
        jnp.bfloat16
    )
    gate_up_held, gate_up_trail = reduce_owner(gate_up, fsdp_order + ctx_order)
    gate_up_sum = spread_owner(gate_up_held, gate_up_trail)[0]
    gate_up_peer = swap(gate_up_sum, "ctx", 0)
    grad_w_gate = jnp.where(core == 0, gate_up_sum, gate_up_peer).astype(jnp.float32)
    grad_w_up = jnp.where(core == 0, gate_up_peer, gate_up_sum).astype(jnp.float32)
    grad_resid, grad_ffn_gain_term = norm_back(part, residual, inverse_two, gain_ffn)
    grad_resid = grad_resid + grad_z.astype(jnp.float32)
    grad_attn_low = grad_resid.astype(jnp.bfloat16)
    out_held, out_trail = reduce_owner(
        by_owner(mixed_low, grad_attn_low), core_order + fsdp_order + ctx_order
    )
    grad_w_out = spread_owner(out_held, out_trail)[0].astype(jnp.float32)
    grad_mixed = (
        contract_cols(grad_attn_low, out_full)
        .astype(jnp.bfloat16)
        .reshape(local_rows, KV_HEADS, group_size, HEAD)
    )
    delta_all = jnp.moveaxis(jnp.sum(grad_mixed.astype(jnp.float32) * mixed_full, axis=-1), 0, -1)
    zero_keys = jnp.zeros((seq_length, KV_HEADS, HEAD), jnp.float32)
    grad_keys_nat, grad_values_nat = (zero_keys, zero_keys)
    query_grads = []
    for half_index in range(2):
        low_row = half_index * half_rows
        high_row = low_row + half_rows
        grad_query_part, grad_keys_nat, grad_values_nat = block_backward(
            queries[low_row:high_row],
            own_pos[low_row:high_row],
            keys_natural,
            values_natural,
            tile_counts[half_index],
            key_span,
            score_scale,
            stat_parts[half_index][0],
            stat_parts[half_index][1],
            grad_mixed[low_row:high_row],
            delta_all[..., low_row:high_row],
            grad_keys_nat,
            grad_values_nat,
        )
        query_grads.append(grad_query_part)
    grad_query_rot = (jnp.concatenate(query_grads, axis=0) * score_scale).reshape(
        local_rows, HEADS, HEAD
    )
    grad_query_low = (
        unrotate(grad_query_rot, cosine_table, sine_table)
        .astype(jnp.bfloat16)
        .reshape(local_rows, HEADS * HEAD)
    )
    grad_both_nat = jnp.concatenate(
        [
            (grad_keys_nat * score_scale).reshape(seq_length, kv_size),
            grad_values_nat.reshape(seq_length, kv_size),
        ],
        axis=1,
    ).astype(jnp.bfloat16)
    held = reorder_blocks(grad_both_nat, device_order, half_rows).reshape(
        pair_total, local_rows, 2 * kv_size
    )
    for bit in range(ctx_bits):
        pairs = held.reshape((held.shape[0] // 2, 2) + held.shape[1:])
        kept = pairs[:, 0].astype(jnp.float32) + swap(pairs[:, 1], "ctx", bit).astype(jnp.float32)
        held = kept.astype(jnp.bfloat16) if bit < ctx_bits - 1 else kept
    key_sum = held[0][:, :kv_size]
    value_sum = held[0][:, kv_size:]
    grad_key_low = (
        unrotate(key_sum.reshape(local_rows, KV_HEADS, HEAD), cosine_table, sine_table)
        .astype(jnp.bfloat16)
        .reshape(local_rows, KV_HEADS * HEAD)
    )
    grad_value_low = value_sum.astype(jnp.bfloat16)
    grad_qkv_low = jnp.concatenate([grad_query_low, grad_key_low, grad_value_low], axis=1)
    grad_normed_one = contract_cols(grad_qkv_low, qkv_full)
    grad_inputs, grad_attn_gain_term = norm_back(grad_normed_one, inputs, inverse_one, gain_attn)
    grad_in = (grad_resid + grad_inputs)[None]
    rows_owned = attn_gain.shape[0]
    gain_terms = jnp.stack([grad_attn_gain_term, grad_ffn_gain_term], axis=1).astype(jnp.bfloat16)
    qkv_product = by_owner(normed_one, grad_qkv_low)
    padding = -(qkv_size + 2) % 256
    qkv_parts = jnp.concatenate(
        [
            qkv_product,
            gain_terms.reshape(owners, rows_owned, 2),
            jnp.zeros((owners, rows_owned, padding), jnp.bfloat16),
        ],
        axis=2,
    )
    qkv_held, qkv_trail = reduce_owner(qkv_parts, core_order + fsdp_order + ctx_order)
    qkv_sum = spread_owner(qkv_held, qkv_trail)[0].astype(jnp.float32)
    return (
        block_out,
        grad_in,
        qkv_sum[:, qkv_size],
        qkv_sum[:, :q_size],
        qkv_sum[:, q_size : q_size + kv_size],
        qkv_sum[:, q_size + kv_size : qkv_size],
        grad_w_out,
        qkv_sum[:, qkv_size + 1],
        grad_w_gate,
        grad_w_up,
        grad_down,
    )


def solution(mesh):
    placed = (
        P("fsdp", "ctx", None),
        P("fsdp", None),
        P("fsdp"),
        P("fsdp", None),
        P("fsdp", None),
        P("fsdp", None),
        P("fsdp", None),
        P("fsdp"),
        P("fsdp", None),
        P("fsdp", None),
        P("fsdp", None),
        P("fsdp", "ctx", None),
    )
    return jax.shard_map(
        body,
        mesh=mesh,
        in_specs=placed,
        out_specs=(
            P("fsdp", "ctx", None),
            P("fsdp", "ctx", None),
            P("fsdp"),
            P("fsdp", None),
            P("fsdp", None),
            P("fsdp", None),
            P("fsdp", None),
            P("fsdp"),
            P("fsdp", None),
            P("fsdp", None),
            P("fsdp", None),
        ),
        check_vma=False,
    )
```

```python
import math

import jax
import jax.numpy as jnp
from jax import lax
from jax.experimental import pallas as pl
from jax.experimental.pallas import tpu as pltpu
from jax.sharding import PartitionSpec as P

HEADS = 15
KV_HEADS = 5
HEAD = 64


NORM_EPS = 1e-05
ROPE_BASE = 100000.0
MASKED = -1e30


def matmul(left_mat, right_mat):
    return jnp.dot(left_mat, right_mat, preferred_element_type=jnp.float32)


def contract_rows(left_mat, right_mat):
    return lax.dot_general(
        left_mat, right_mat, (((0,), (0,)), ((), ())), preferred_element_type=jnp.float32
    )


def contract_cols(left_mat, right_mat):
    return lax.dot_general(
        left_mat, right_mat, (((1,), (1,)), ((), ())), preferred_element_type=jnp.float32
    )


def rope_tables(positions, head_size):
    half_size = head_size // 2
    exponent = jnp.arange(half_size, dtype=jnp.float32) * (2.0 / head_size)
    frequency = jnp.exp(-exponent * math.log(ROPE_BASE))
    angle_table = positions.astype(jnp.float32)[:, None] * frequency[None, :]
    return (jnp.cos(angle_table)[:, None, :], jnp.sin(angle_table)[:, None, :])


def rotate(vectors, cosine_table, sine_table):
    half_size = vectors.shape[-1] // 2
    front_half = vectors[..., :half_size]
    back_half = vectors[..., half_size:]
    return jnp.concatenate(
        [
            front_half * cosine_table - back_half * sine_table,
            back_half * cosine_table + front_half * sine_table,
        ],
        axis=-1,
    )


def unrotate(grad_vec, cosine_table, sine_table):
    half_size = grad_vec.shape[-1] // 2
    front_half = grad_vec[..., :half_size]
    back_half = grad_vec[..., half_size:]
    return jnp.concatenate(
        [
            front_half * cosine_table + back_half * sine_table,
            back_half * cosine_table - front_half * sine_table,
        ],
        axis=-1,
    )


def inverse_rms(source):
    return lax.rsqrt(jnp.mean(source * source, axis=-1, keepdims=True) + NORM_EPS)


def norm_back(grad_normed, source, inverse, gain_vec):
    scaled = grad_normed * gain_vec
    inner = jnp.sum(scaled * source, axis=-1, keepdims=True) / source.shape[-1]
    grad_source = inverse * scaled - source * (inverse * inverse * inverse) * inner
    grad_gain = jnp.sum(grad_normed * source * inverse, axis=0)
    return (grad_source, grad_gain)


def tie_kernel(value_ref, after_ref, out_ref):
    del value_ref, after_ref, out_ref


def tie(value, after):
    anywhere = pl.BlockSpec(memory_space=pl.ANY)
    return pl.pallas_call(
        tie_kernel,
        out_shape=jax.ShapeDtypeStruct(value.shape, value.dtype),
        in_specs=[anywhere, anywhere],
        out_specs=anywhere,
        input_output_aliases={0: 0},
        name="tie",
    )(value, after)


def masked_scores(query_ref, key_ref, query_pos_ref, key_pos_ref):
    scores = contract_cols(query_ref[0], key_ref[0]) * HEAD ** (-0.5)
    return jnp.where(key_pos_ref[...] <= query_pos_ref[...], scores, MASKED)


def forward_kernel(query_ref, key_ref, value_ref, query_pos_ref, key_pos_ref, mixed_ref, lse_ref):
    scores = masked_scores(query_ref, key_ref, query_pos_ref, key_pos_ref)
    row_max = jnp.max(scores, axis=-1, keepdims=True)
    weights = jnp.exp(scores - row_max)
    row_sum = jnp.sum(weights, axis=-1, keepdims=True)
    weights = (weights * (1.0 / row_sum)).astype(jnp.bfloat16)
    mixed_ref[0] = matmul(weights, value_ref[0])
    lse_ref[0] = row_max + jnp.log(row_sum)


def backward_kernel(
    query_ref,
    key_ref,
    value_ref,
    query_pos_ref,
    key_pos_ref,
    lse_ref,
    mixed_ref,
    grad_mixed_ref,
    after_ref,
    other_after_ref,
    grad_query_ref,
    grad_key_ref,
    grad_value_ref,
):
    del after_ref, other_after_ref
    scores = masked_scores(query_ref, key_ref, query_pos_ref, key_pos_ref)
    probs = jnp.exp(scores - lse_ref[0])
    grad_mixed = grad_mixed_ref[0]
    delta = jnp.sum(grad_mixed.astype(jnp.float32) * mixed_ref[0], axis=-1, keepdims=True)
    grad_value_ref[0] = contract_rows(probs.astype(jnp.bfloat16), grad_mixed).astype(jnp.bfloat16)
    grad_probs = contract_cols(grad_mixed, value_ref[0])
    grad_scores = (probs * (grad_probs - delta)).astype(jnp.bfloat16)
    grad_query_ref[0] = matmul(grad_scores, key_ref[0]) * HEAD ** (-0.5)
    grad_key_ref[0] = (contract_rows(grad_scores, query_ref[0]) * HEAD ** (-0.5)).astype(
        jnp.bfloat16
    )


def per_head(rows, columns):
    return pl.BlockSpec((1, rows, columns), lambda head: (head, 0, 0))


def shared(rows, columns):
    return pl.BlockSpec((rows, columns), lambda head: (0, 0))


def attend_forward(queries, keys, values, query_pos, key_pos):
    heads, rows, _ = queries.shape
    length = keys.shape[1]
    return pl.pallas_call(
        forward_kernel,
        grid=(heads,),
        in_specs=[
            per_head(rows, HEAD),
            per_head(length, HEAD),
            per_head(length, HEAD),
            shared(rows, 1),
            shared(1, length),
        ],
        out_specs=[per_head(rows, HEAD), per_head(rows, 1)],
        out_shape=[
            jax.ShapeDtypeStruct((heads, rows, HEAD), jnp.float32),
            jax.ShapeDtypeStruct((heads, rows, 1), jnp.float32),
        ],
        compiler_params=pltpu.CompilerParams(vmem_limit_bytes=50 * 2**20),
        cost_estimate=pl.CostEstimate(
            flops=8 * heads * rows * length * HEAD,
            bytes_accessed=8 * heads * length * HEAD,
            transcendentals=heads * rows * length,
        ),
        name="attend_forward",
    )(queries, keys, values, query_pos, key_pos)


def attend_backward(
    queries, keys, values, query_pos, key_pos, lse, mixed, grad_mixed, after, other_after
):
    heads, rows, _ = queries.shape
    length = keys.shape[1]
    anywhere = pl.BlockSpec(memory_space=pl.ANY)
    return pl.pallas_call(
        backward_kernel,
        grid=(heads,),
        in_specs=[
            per_head(rows, HEAD),
            per_head(length, HEAD),
            per_head(length, HEAD),
            shared(rows, 1),
            shared(1, length),
            per_head(rows, 1),
            per_head(rows, HEAD),
            per_head(rows, HEAD),
            anywhere,
            anywhere,
        ],
        out_specs=[per_head(rows, HEAD), per_head(length, HEAD), per_head(length, HEAD)],
        out_shape=[
            jax.ShapeDtypeStruct((heads, rows, HEAD), jnp.float32),
            jax.ShapeDtypeStruct((heads, length, HEAD), jnp.bfloat16),
            jax.ShapeDtypeStruct((heads, length, HEAD), jnp.bfloat16),
        ],
        compiler_params=pltpu.CompilerParams(vmem_limit_bytes=50 * 2**20),
        cost_estimate=pl.CostEstimate(
            flops=40 * heads * rows * length * HEAD,
            bytes_accessed=16 * heads * length * HEAD,
            transcendentals=heads * rows * length,
        ),
        name="attend_backward",
    )(queries, keys, values, query_pos, key_pos, lse, mixed, grad_mixed, after, other_after)


def bit_of(axis_name, bit):
    return (lax.axis_index(axis_name) >> bit) & 1


def swap(array, axis_name, bit):
    size = lax.axis_size(axis_name)
    return lax.ppermute(array, axis_name, [(i, i ^ (1 << bit)) for i in range(size)])


def bits_of(axis_name):
    return lax.axis_size(axis_name).bit_length() - 1


def half_of(array, index, dim):
    size = array.shape[dim] // 2
    return lax.dynamic_slice_in_dim(array, index * size, size, dim)


def join(mine, other, bit, dim):
    first = jnp.where(bit == 0, mine, other)
    second = jnp.where(bit == 0, other, mine)
    return jnp.concatenate([first, second], axis=dim)


def gather_weight(shard, after=None):
    core = bit_of("ctx", 0)
    part = half_of(shard, core, 0)[None]
    if after is not None:
        part = tie(part, after)
    size = lax.axis_size("fsdp")
    pieces = [
        lax.ppermute(part, "fsdp", [(i, (i + step) % size) for i in range(size)])
        for step in range(1, size)
    ]
    pieces = [join(piece, swap(piece, "ctx", 0), core, 1) for piece in pieces]
    own = lax.axis_index("fsdp")
    rows = shard.shape[0]
    if size == 2:
        return join(shard, pieces[0][0], own, 0)
    full = jnp.zeros((size * rows,) + shard.shape[1:], shard.dtype)
    full = lax.dynamic_update_slice_in_dim(full, shard, own * rows, 0)
    for step, piece in enumerate(pieces):
        source = (own - step - 1 + size) % size
        full = lax.dynamic_update_slice_in_dim(full, piece[0], source * rows, 0)
    return full


def split_dim(shape):
    rows, columns = shape[1], shape[2]
    if rows % 16 == 0:
        return 1
    if columns % 256 == 0 or rows % 2:
        return 2
    return 1 if columns % 2 else 2


def reduce_owner(parts, order):
    trail = []
    held = parts
    for axis_name, bit in order:
        dim = 0 if axis_name == "fsdp" else split_dim(held.shape)
        own = bit_of(axis_name, bit)
        other = swap(half_of(held, 1 - own, dim), axis_name, bit)
        kept = half_of(held, own, dim)
        held = (kept.astype(jnp.float32) + other.astype(jnp.float32)).astype(jnp.bfloat16)
        if axis_name == "ctx":
            trail.append((bit, dim))
    return held, trail


def spread_owner(held, trail):
    for bit, dim in reversed(trail):
        held = join(held, swap(held, "ctx", bit), bit_of("ctx", bit), dim)
    return held


def orders():
    fsdp = [("fsdp", bit) for bit in reversed(range(bits_of("fsdp")))]
    ctx = [("ctx", bit) for bit in range(1, bits_of("ctx"))]
    return fsdp, ctx


def body(
    tokens,
    pair_of,
    attn_gain,
    w_query,
    w_key,
    w_value,
    w_out,
    ffn_gain,
    w_gate,
    w_up,
    w_down,
    out_grad,
):
    inputs = tokens[0].astype(jnp.float32)
    local_rows = inputs.shape[0]
    half_rows = local_rows // 2
    pair_row = pair_of[0]
    pair_total = lax.axis_size("ctx")
    seq_length = pair_total * local_rows
    group_size = HEADS // KV_HEADS
    first_bundle = jnp.concatenate(
        [w_query, w_key, w_value, attn_gain[:, None], ffn_gain[:, None]], axis=1
    )
    first_full = gather_weight(first_bundle)
    kv_size = KV_HEADS * HEAD
    q_size = HEADS * HEAD
    qkv_size = q_size + 2 * kv_size
    qkv_full = first_full[:, :qkv_size]
    gain_attn = first_full[:, qkv_size]
    gain_ffn = first_full[:, qkv_size + 1]
    out_full = gather_weight(w_out, first_full)
    gate_full = gather_weight(w_gate, first_full)
    up_full = gather_weight(w_up, first_full)
    down_full = gather_weight(w_down, first_full)
    gain_attn = gain_attn.astype(jnp.float32)
    gain_ffn = gain_ffn.astype(jnp.float32)
    slot_ids = jnp.arange(pair_total, dtype=jnp.int32)
    own_pair = jnp.sum(jnp.where(slot_ids == lax.axis_index("ctx"), pair_row, 0))
    own_blocks = jnp.stack([own_pair, 2 * pair_total - 1 - own_pair])
    offsets = jnp.arange(half_rows, dtype=jnp.int32)
    own_pos = (own_blocks[:, None] * half_rows + offsets[None, :]).reshape(local_rows)
    cosine_table, sine_table = rope_tables(own_pos, HEAD)
    partner = slot_ids ^ lax.axis_index("ctx")
    relative_pair = jnp.sum(
        jnp.where(partner[:, None] == slot_ids[None, :], pair_row[None, :], 0), axis=1
    )
    relative_blocks = jnp.stack(
        [relative_pair, 2 * pair_total - 1 - relative_pair], axis=1
    ).reshape(2 * pair_total)
    key_pos = (relative_blocks[:, None] * half_rows + offsets[None, :]).reshape(1, seq_length)
    query_pos = jnp.tile(own_pos, group_size)[:, None]
    inverse_one = inverse_rms(inputs)
    normed_one = (inputs * inverse_one * gain_attn).astype(jnp.bfloat16)
    raw_all = matmul(normed_one, qkv_full)
    query_raw = raw_all[:, :q_size].reshape(local_rows, HEADS, HEAD)
    key_raw = raw_all[:, q_size : q_size + kv_size].reshape(local_rows, KV_HEADS, HEAD)
    value_local = raw_all[:, q_size + kv_size :].astype(jnp.bfloat16)
    def grouped(rows_in):
        return jnp.moveaxis(rows_in.reshape(local_rows, HEADS, HEAD), 0, 1).reshape(
            KV_HEADS, group_size * local_rows, HEAD
        )

    def ungrouped(heads_in):
        return jnp.moveaxis(heads_in.reshape(HEADS, local_rows, HEAD), 0, 1)

    queries = grouped(rotate(query_raw, cosine_table, sine_table).astype(jnp.bfloat16))
    key_local = (
        rotate(key_raw, cosine_table, sine_table)
        .astype(jnp.bfloat16)
        .reshape(local_rows, KV_HEADS * HEAD)
    )
    ctx_bits = bits_of("ctx")
    both = jnp.concatenate([key_local, value_local], axis=1)[None]
    for bit in reversed(range(ctx_bits)):
        both = jnp.stack([both, swap(both, "ctx", bit)], axis=1).reshape(
            (2 * both.shape[0],) + both.shape[1:]
        )
    both_heads = jnp.moveaxis(both.reshape(seq_length, 2 * KV_HEADS, HEAD), 0, 1)
    keys = both_heads[:KV_HEADS]
    values = both_heads[KV_HEADS:]
    mixed_full, lse = attend_forward(queries, keys, values, query_pos, key_pos)
    mixed_low = ungrouped(mixed_full).reshape(local_rows, q_size).astype(jnp.bfloat16)
    residual = inputs + matmul(mixed_low, out_full)
    inverse_two = inverse_rms(residual)
    normed_two = (residual * inverse_two * gain_ffn).astype(jnp.bfloat16)
    columns = normed_two
    gate_pre = matmul(columns, gate_full)
    up_pre = matmul(columns, up_full)
    sigmoid_gate = jax.nn.sigmoid(gate_pre)
    activated = gate_pre * sigmoid_gate
    hidden = (activated * up_pre).astype(jnp.bfloat16)
    columns = hidden
    down_out = matmul(columns, down_full)
    block_out = (residual + down_out).astype(jnp.bfloat16)[None]
    grad_z = out_grad[0]
    grad_hidden = contract_cols(grad_z, down_full)
    grad_gate_low = (
        grad_hidden * up_pre * sigmoid_gate * (1.0 + gate_pre * (1.0 - sigmoid_gate))
    ).astype(jnp.bfloat16)
    grad_up_low = (grad_hidden * activated).astype(jnp.bfloat16)
    part = contract_cols(grad_gate_low, gate_full) + contract_cols(grad_up_low, up_full)
    owners = lax.axis_size("fsdp")
    core = bit_of("ctx", 0)
    fsdp_order, ctx_order = orders()
    core_order = [("ctx", 0)]

    def by_owner(left_mat, right_mat):
        product = contract_rows(left_mat, right_mat).astype(jnp.bfloat16)
        return product.reshape((owners, product.shape[0] // owners, product.shape[1]))

    down_product = by_owner(hidden, grad_z)
    down_held, down_trail = reduce_owner(
        down_product, core_order + fsdp_order + ctx_order
    )
    grad_down = spread_owner(down_held, down_trail)[0].astype(jnp.float32)
    gate_up_other = swap(
        by_owner(normed_two, jnp.where(core == 0, grad_up_low, grad_gate_low)), "ctx", 0
    )
    gate_up_mine = by_owner(normed_two, jnp.where(core == 0, grad_gate_low, grad_up_low))
    gate_up = (gate_up_mine.astype(jnp.float32) + gate_up_other.astype(jnp.float32)).astype(
        jnp.bfloat16
    )
    ff_half = gate_up.shape[2] // 2
    gate_up_sums = []
    for part_index, part_order in enumerate((fsdp_order + ctx_order, ctx_order + fsdp_order)):
        columns = gate_up[:, :, part_index * ff_half : (part_index + 1) * ff_half]
        gate_up_held, gate_up_trail = reduce_owner(columns, part_order)
        gate_up_sums.append(spread_owner(gate_up_held, gate_up_trail)[0])
    gate_up_sum = jnp.concatenate(gate_up_sums, axis=1)
    gate_up_peer = swap(gate_up_sum, "ctx", 0)
    grad_w_gate = jnp.where(core == 0, gate_up_sum, gate_up_peer).astype(jnp.float32)
    grad_w_up = jnp.where(core == 0, gate_up_peer, gate_up_sum).astype(jnp.float32)
    grad_resid, grad_ffn_gain_term = norm_back(part, residual, inverse_two, gain_ffn)
    grad_resid = grad_resid + grad_z.astype(jnp.float32)
    grad_attn_low = grad_resid.astype(jnp.bfloat16)
    out_held, out_trail = reduce_owner(
        by_owner(mixed_low, grad_attn_low), core_order + fsdp_order + ctx_order
    )
    grad_w_out = spread_owner(out_held, out_trail)[0].astype(jnp.float32)
    grad_mixed = grouped(contract_cols(grad_attn_low, out_full).astype(jnp.bfloat16))
    grad_queries, grad_keys, grad_values = attend_backward(
        queries,
        keys,
        values,
        query_pos,
        key_pos,
        lse,
        mixed_full,
        grad_mixed,
        gate_up,
        down_product,
    )
    grad_query_rot = ungrouped(grad_queries)
    grad_query_low = (
        unrotate(grad_query_rot, cosine_table, sine_table)
        .astype(jnp.bfloat16)
        .reshape(local_rows, HEADS * HEAD)
    )
    held = jnp.moveaxis(jnp.concatenate([grad_keys, grad_values], axis=0), 0, 1).reshape(
        pair_total, local_rows, 2 * kv_size
    )
    for bit in range(ctx_bits):
        pairs = held.reshape((held.shape[0] // 2, 2) + held.shape[1:])
        kept = pairs[:, 0].astype(jnp.float32) + swap(pairs[:, 1], "ctx", bit).astype(jnp.float32)
        held = kept.astype(jnp.bfloat16) if bit < ctx_bits - 1 else kept
    key_sum = held[0][:, :kv_size]
    value_sum = held[0][:, kv_size:]
    grad_key_low = (
        unrotate(key_sum.reshape(local_rows, KV_HEADS, HEAD), cosine_table, sine_table)
        .astype(jnp.bfloat16)
        .reshape(local_rows, KV_HEADS * HEAD)
    )
    grad_value_low = value_sum.astype(jnp.bfloat16)
    grad_qkv_low = jnp.concatenate([grad_query_low, grad_key_low, grad_value_low], axis=1)
    grad_normed_one = contract_cols(grad_qkv_low, qkv_full)
    grad_inputs, grad_attn_gain_term = norm_back(grad_normed_one, inputs, inverse_one, gain_attn)
    grad_in = (grad_resid + grad_inputs)[None]
    rows_owned = attn_gain.shape[0]
    gain_terms = jnp.stack([grad_attn_gain_term, grad_ffn_gain_term], axis=1).astype(jnp.bfloat16)
    qkv_product = by_owner(normed_one, grad_qkv_low)
    padding = -(qkv_size + 2) % 256
    qkv_parts = jnp.concatenate(
        [
            qkv_product,
            gain_terms.reshape(owners, rows_owned, 2),
            jnp.zeros((owners, rows_owned, padding), jnp.bfloat16),
        ],
        axis=2,
    )
    qkv_held, qkv_trail = reduce_owner(qkv_parts, core_order + fsdp_order + ctx_order)
    qkv_sum = spread_owner(qkv_held, qkv_trail)[0].astype(jnp.float32)
    return (
        block_out,
        grad_in,
        qkv_sum[:, qkv_size],
        qkv_sum[:, :q_size],
        qkv_sum[:, q_size : q_size + kv_size],
        qkv_sum[:, q_size + kv_size : qkv_size],
        grad_w_out,
        qkv_sum[:, qkv_size + 1],
        grad_w_gate,
        grad_w_up,
        grad_down,
    )


def solution(mesh):
    placed = (
        P("fsdp", "ctx", None),
        P("fsdp", None),
        P("fsdp"),
        P("fsdp", None),
        P("fsdp", None),
        P("fsdp", None),
        P("fsdp", None),
        P("fsdp"),
        P("fsdp", None),
        P("fsdp", None),
        P("fsdp", None),
        P("fsdp", "ctx", None),
    )
    return jax.shard_map(
        body,
        mesh=mesh,
        in_specs=placed,
        out_specs=(
            P("fsdp", "ctx", None),
            P("fsdp", "ctx", None),
            P("fsdp"),
            P("fsdp", None),
            P("fsdp", None),
            P("fsdp", None),
            P("fsdp", None),
            P("fsdp"),
            P("fsdp", None),
            P("fsdp", None),
            P("fsdp", None),
        ),
        check_vma=False,
    )
```

```python
import math

import jax
import jax.numpy as jnp
from jax import lax
from jax.experimental import pallas as pl
from jax.experimental.pallas import tpu as pltpu
from jax.sharding import PartitionSpec as P

HEADS = 15
KV_HEADS = 5
HEAD = 64


NORM_EPS = 1e-05
ROPE_BASE = 100000.0
MASKED = -1e30


def matmul(left_mat, right_mat):
    return jnp.dot(left_mat, right_mat, preferred_element_type=jnp.float32)


def contract_rows(left_mat, right_mat):
    return lax.dot_general(
        left_mat, right_mat, (((0,), (0,)), ((), ())), preferred_element_type=jnp.float32
    )


def contract_cols(left_mat, right_mat):
    return lax.dot_general(
        left_mat, right_mat, (((1,), (1,)), ((), ())), preferred_element_type=jnp.float32
    )


def rope_tables(positions, head_size):
    half_size = head_size // 2
    exponent = jnp.arange(half_size, dtype=jnp.float32) * (2.0 / head_size)
    frequency = jnp.exp(-exponent * math.log(ROPE_BASE))
    angle_table = positions.astype(jnp.float32)[:, None] * frequency[None, :]
    return (jnp.cos(angle_table)[:, None, :], jnp.sin(angle_table)[:, None, :])


def rotate(vectors, cosine_table, sine_table):
    half_size = vectors.shape[-1] // 2
    front_half = vectors[..., :half_size]
    back_half = vectors[..., half_size:]
    return jnp.concatenate(
        [
            front_half * cosine_table - back_half * sine_table,
            back_half * cosine_table + front_half * sine_table,
        ],
        axis=-1,
    )


def unrotate(grad_vec, cosine_table, sine_table):
    half_size = grad_vec.shape[-1] // 2
    front_half = grad_vec[..., :half_size]
    back_half = grad_vec[..., half_size:]
    return jnp.concatenate(
        [
            front_half * cosine_table + back_half * sine_table,
            back_half * cosine_table - front_half * sine_table,
        ],
        axis=-1,
    )


def inverse_rms(source):
    return lax.rsqrt(jnp.mean(source * source, axis=-1, keepdims=True) + NORM_EPS)


def norm_back(grad_normed, source, inverse, gain_vec):
    scaled = grad_normed * gain_vec
    inner = jnp.sum(scaled * source, axis=-1, keepdims=True) / source.shape[-1]
    grad_source = inverse * scaled - source * (inverse * inverse * inverse) * inner
    grad_gain = jnp.sum(grad_normed * source * inverse, axis=0)
    return (grad_source, grad_gain)


def tie_kernel(value_ref, after_ref, out_ref):
    del value_ref, after_ref, out_ref


def tie(value, after):
    anywhere = pl.BlockSpec(memory_space=pl.ANY)
    return pl.pallas_call(
        tie_kernel,
        out_shape=jax.ShapeDtypeStruct(value.shape, value.dtype),
        in_specs=[anywhere, anywhere],
        out_specs=anywhere,
        input_output_aliases={0: 0},
        name="tie",
    )(value, after)


def masked_scores(query_ref, key_ref, query_pos_ref, key_pos_ref):
    scores = contract_cols(query_ref[0], key_ref[0]) * HEAD ** (-0.5)
    return jnp.where(key_pos_ref[...] <= query_pos_ref[...], scores, MASKED)


def forward_kernel(query_ref, key_ref, value_ref, query_pos_ref, key_pos_ref, mixed_ref, lse_ref):
    scores = masked_scores(query_ref, key_ref, query_pos_ref, key_pos_ref)
    row_max = jnp.max(scores, axis=-1, keepdims=True)
    weights = jnp.exp(scores - row_max)
    row_sum = jnp.sum(weights, axis=-1, keepdims=True)
    weights = (weights * (1.0 / row_sum)).astype(jnp.bfloat16)
    mixed_ref[0] = matmul(weights, value_ref[0])
    lse_ref[0] = row_max + jnp.log(row_sum)


def backward_kernel(
    query_ref,
    key_ref,
    value_ref,
    query_pos_ref,
    key_pos_ref,
    lse_ref,
    mixed_ref,
    grad_mixed_ref,
    after_ref,
    other_after_ref,
    grad_query_ref,
    grad_key_ref,
    grad_value_ref,
):
    del after_ref, other_after_ref
    scores = masked_scores(query_ref, key_ref, query_pos_ref, key_pos_ref)
    probs = jnp.exp(scores - lse_ref[0])
    grad_mixed = grad_mixed_ref[0]
    delta = jnp.sum(grad_mixed.astype(jnp.float32) * mixed_ref[0], axis=-1, keepdims=True)
    grad_value_ref[0] = contract_rows(probs.astype(jnp.bfloat16), grad_mixed).astype(jnp.bfloat16)
    grad_probs = contract_cols(grad_mixed, value_ref[0])
    grad_scores = (probs * (grad_probs - delta)).astype(jnp.bfloat16)
    grad_query_ref[0] = matmul(grad_scores, key_ref[0]) * HEAD ** (-0.5)
    grad_key_ref[0] = (contract_rows(grad_scores, query_ref[0]) * HEAD ** (-0.5)).astype(
        jnp.bfloat16
    )


def per_head(rows, columns):
    return pl.BlockSpec((1, rows, columns), lambda head: (head, 0, 0))


def shared(rows, columns):
    return pl.BlockSpec((rows, columns), lambda head: (0, 0))


def attend_forward(queries, keys, values, query_pos, key_pos):
    heads, rows, _ = queries.shape
    length = keys.shape[1]
    return pl.pallas_call(
        forward_kernel,
        grid=(heads,),
        in_specs=[
            per_head(rows, HEAD),
            per_head(length, HEAD),
            per_head(length, HEAD),
            shared(rows, 1),
            shared(1, length),
        ],
        out_specs=[per_head(rows, HEAD), per_head(rows, 1)],
        out_shape=[
            jax.ShapeDtypeStruct((heads, rows, HEAD), jnp.float32),
            jax.ShapeDtypeStruct((heads, rows, 1), jnp.float32),
        ],
        compiler_params=pltpu.CompilerParams(vmem_limit_bytes=50 * 2**20),
        cost_estimate=pl.CostEstimate(
            flops=8 * heads * rows * length * HEAD,
            bytes_accessed=8 * heads * length * HEAD,
            transcendentals=heads * rows * length,
        ),
        name="attend_forward",
    )(queries, keys, values, query_pos, key_pos)


def attend_backward(
    queries, keys, values, query_pos, key_pos, lse, mixed, grad_mixed, after, other_after
):
    heads, rows, _ = queries.shape
    length = keys.shape[1]
    anywhere = pl.BlockSpec(memory_space=pl.ANY)
    return pl.pallas_call(
        backward_kernel,
        grid=(heads,),
        in_specs=[
            per_head(rows, HEAD),
            per_head(length, HEAD),
            per_head(length, HEAD),
            shared(rows, 1),
            shared(1, length),
            per_head(rows, 1),
            per_head(rows, HEAD),
            per_head(rows, HEAD),
            anywhere,
            anywhere,
        ],
        out_specs=[per_head(rows, HEAD), per_head(length, HEAD), per_head(length, HEAD)],
        out_shape=[
            jax.ShapeDtypeStruct((heads, rows, HEAD), jnp.float32),
            jax.ShapeDtypeStruct((heads, length, HEAD), jnp.bfloat16),
            jax.ShapeDtypeStruct((heads, length, HEAD), jnp.bfloat16),
        ],
        compiler_params=pltpu.CompilerParams(vmem_limit_bytes=50 * 2**20),
        cost_estimate=pl.CostEstimate(
            flops=40 * heads * rows * length * HEAD,
            bytes_accessed=16 * heads * length * HEAD,
            transcendentals=heads * rows * length,
        ),
        name="attend_backward",
    )(queries, keys, values, query_pos, key_pos, lse, mixed, grad_mixed, after, other_after)


def bit_of(axis_name, bit):
    return (lax.axis_index(axis_name) >> bit) & 1


def swap(array, axis_name, bit):
    size = lax.axis_size(axis_name)
    return lax.ppermute(array, axis_name, [(i, i ^ (1 << bit)) for i in range(size)])


def bits_of(axis_name):
    return lax.axis_size(axis_name).bit_length() - 1


def half_of(array, index, dim):
    size = array.shape[dim] // 2
    return lax.dynamic_slice_in_dim(array, index * size, size, dim)


def join(mine, other, bit, dim):
    first = jnp.where(bit == 0, mine, other)
    second = jnp.where(bit == 0, other, mine)
    return jnp.concatenate([first, second], axis=dim)


def gather_weight(shard):
    core = bit_of("ctx", 0)
    part = half_of(shard, core, 0)[None]
    size = lax.axis_size("fsdp")
    pieces = [
        lax.ppermute(part, "fsdp", [(i, (i + step) % size) for i in range(size)])
        for step in range(1, size)
    ]
    return pieces


def finish_weight(shard, pieces, after=None):
    core = bit_of("ctx", 0)
    size = lax.axis_size("fsdp")
    if after is not None:
        pieces = [tie(piece, after) for piece in pieces]
    pieces = [join(piece, swap(piece, "ctx", 0), core, 1) for piece in pieces]
    own = lax.axis_index("fsdp")
    rows = shard.shape[0]
    if size == 2:
        return join(shard, pieces[0][0], own, 0)
    full = jnp.zeros((size * rows,) + shard.shape[1:], shard.dtype)
    full = lax.dynamic_update_slice_in_dim(full, shard, own * rows, 0)
    for step, piece in enumerate(pieces):
        source = (own - step - 1 + size) % size
        full = lax.dynamic_update_slice_in_dim(full, piece[0], source * rows, 0)
    return full


def split_dim(shape):
    rows, columns = shape[1], shape[2]
    if rows % 16 == 0:
        return 1
    if columns % 256 == 0 or rows % 2:
        return 2
    return 1 if columns % 2 else 2


def reduce_open(held, order):
    axis_name, bit = order[0]
    dim = 0 if axis_name == "fsdp" else split_dim(held.shape)
    own = bit_of(axis_name, bit)
    sent = half_of(held, 1 - own, dim)
    return half_of(held, own, dim), sent, swap(sent, axis_name, bit), dim


def add_low(kept, other):
    return (kept.astype(jnp.float32) + other.astype(jnp.float32)).astype(jnp.bfloat16)


def reduce_owner(opened, order, after=None):
    trail = []
    kept, _, other, dim = opened
    if after is not None:
        other = tie(other, after)
    for index, (axis_name, bit) in enumerate(order):
        if index:
            kept, _, other, dim = reduce_open(held, order[index:])
        held = add_low(kept, other)
        if axis_name == "ctx":
            trail.append((bit, dim))
    return held, trail


def spread_owner(held, trail):
    for bit, dim in reversed(trail):
        held = join(held, swap(held, "ctx", bit), bit_of("ctx", bit), dim)
    return held


def orders():
    fsdp = [("fsdp", bit) for bit in reversed(range(bits_of("fsdp")))]
    ctx = [("ctx", bit) for bit in range(1, bits_of("ctx"))]
    return fsdp, ctx


def body(
    tokens,
    pair_of,
    attn_gain,
    w_query,
    w_key,
    w_value,
    w_out,
    ffn_gain,
    w_gate,
    w_up,
    w_down,
    out_grad,
):
    inputs = tokens[0].astype(jnp.float32)
    local_rows = inputs.shape[0]
    half_rows = local_rows // 2
    pair_row = pair_of[0]
    pair_total = lax.axis_size("ctx")
    seq_length = pair_total * local_rows
    group_size = HEADS // KV_HEADS
    first_bundle = jnp.concatenate(
        [w_query, w_key, w_value, attn_gain[:, None], ffn_gain[:, None]], axis=1
    )
    first_full = finish_weight(first_bundle, gather_weight(first_bundle))
    kv_size = KV_HEADS * HEAD
    q_size = HEADS * HEAD
    qkv_size = q_size + 2 * kv_size
    qkv_full = first_full[:, :qkv_size]
    gain_attn = first_full[:, qkv_size]
    gain_ffn = first_full[:, qkv_size + 1]
    out_full = finish_weight(w_out, gather_weight(w_out))
    later_weights = (w_gate, w_up, w_down)
    later_pieces = [gather_weight(weight) for weight in later_weights]
    gain_attn = gain_attn.astype(jnp.float32)
    gain_ffn = gain_ffn.astype(jnp.float32)
    slot_ids = jnp.arange(pair_total, dtype=jnp.int32)
    own_pair = jnp.sum(jnp.where(slot_ids == lax.axis_index("ctx"), pair_row, 0))
    own_blocks = jnp.stack([own_pair, 2 * pair_total - 1 - own_pair])
    offsets = jnp.arange(half_rows, dtype=jnp.int32)
    own_pos = (own_blocks[:, None] * half_rows + offsets[None, :]).reshape(local_rows)
    cosine_table, sine_table = rope_tables(own_pos, HEAD)
    partner = slot_ids ^ lax.axis_index("ctx")
    relative_pair = jnp.sum(
        jnp.where(partner[:, None] == slot_ids[None, :], pair_row[None, :], 0), axis=1
    )
    relative_blocks = jnp.stack(
        [relative_pair, 2 * pair_total - 1 - relative_pair], axis=1
    ).reshape(2 * pair_total)
    key_pos = (relative_blocks[:, None] * half_rows + offsets[None, :]).reshape(1, seq_length)
    query_pos = jnp.tile(own_pos, group_size)[:, None]
    inverse_one = inverse_rms(inputs)
    normed_one = (inputs * inverse_one * gain_attn).astype(jnp.bfloat16)
    raw_all = matmul(normed_one, qkv_full)
    query_raw = raw_all[:, :q_size].reshape(local_rows, HEADS, HEAD)
    key_raw = raw_all[:, q_size : q_size + kv_size].reshape(local_rows, KV_HEADS, HEAD)
    value_local = raw_all[:, q_size + kv_size :].astype(jnp.bfloat16)
    def grouped(rows_in):
        return jnp.moveaxis(rows_in.reshape(local_rows, HEADS, HEAD), 0, 1).reshape(
            KV_HEADS, group_size * local_rows, HEAD
        )

    def ungrouped(heads_in):
        return jnp.moveaxis(heads_in.reshape(HEADS, local_rows, HEAD), 0, 1)

    queries = grouped(rotate(query_raw, cosine_table, sine_table).astype(jnp.bfloat16))
    key_local = (
        rotate(key_raw, cosine_table, sine_table)
        .astype(jnp.bfloat16)
        .reshape(local_rows, KV_HEADS * HEAD)
    )
    ctx_bits = bits_of("ctx")
    both = jnp.concatenate([key_local, value_local], axis=1)[None]
    for bit in reversed(range(ctx_bits)):
        both = jnp.stack([both, swap(both, "ctx", bit)], axis=1).reshape(
            (2 * both.shape[0],) + both.shape[1:]
        )
    both_heads = jnp.moveaxis(both.reshape(seq_length, 2 * KV_HEADS, HEAD), 0, 1)
    keys = both_heads[:KV_HEADS]
    values = both_heads[KV_HEADS:]
    mixed_full, lse = attend_forward(queries, keys, values, query_pos, key_pos)
    gate_full, up_full, down_full = [
        finish_weight(weight, pieces, lse) for weight, pieces in zip(later_weights, later_pieces)
    ]
    mixed_low = ungrouped(mixed_full).reshape(local_rows, q_size).astype(jnp.bfloat16)
    residual = inputs + matmul(mixed_low, out_full)
    inverse_two = inverse_rms(residual)
    normed_two = (residual * inverse_two * gain_ffn).astype(jnp.bfloat16)
    columns = normed_two
    gate_pre = matmul(columns, gate_full)
    up_pre = matmul(columns, up_full)
    sigmoid_gate = jax.nn.sigmoid(gate_pre)
    activated = gate_pre * sigmoid_gate
    hidden = (activated * up_pre).astype(jnp.bfloat16)
    columns = hidden
    down_out = matmul(columns, down_full)
    block_out = (residual + down_out).astype(jnp.bfloat16)[None]
    grad_z = out_grad[0]
    grad_hidden = contract_cols(grad_z, down_full)
    grad_gate_low = (
        grad_hidden * up_pre * sigmoid_gate * (1.0 + gate_pre * (1.0 - sigmoid_gate))
    ).astype(jnp.bfloat16)
    grad_up_low = (grad_hidden * activated).astype(jnp.bfloat16)
    part = contract_cols(grad_gate_low, gate_full) + contract_cols(grad_up_low, up_full)
    owners = lax.axis_size("fsdp")
    core = bit_of("ctx", 0)
    fsdp_order, ctx_order = orders()
    core_order = [("ctx", 0)]

    def by_owner(left_mat, right_mat):
        product = contract_rows(left_mat, right_mat).astype(jnp.bfloat16)
        return product.reshape((owners, product.shape[0] // owners, product.shape[1]))

    down_product = by_owner(hidden, grad_z)
    down_kept, _, down_other, down_dim = reduce_open(down_product, core_order)
    down_open = reduce_open(add_low(down_kept, down_other), fsdp_order + ctx_order)
    gate_up_other = swap(
        by_owner(normed_two, jnp.where(core == 0, grad_up_low, grad_gate_low)), "ctx", 0
    )
    gate_up_mine = by_owner(normed_two, jnp.where(core == 0, grad_gate_low, grad_up_low))
    gate_up = (gate_up_mine.astype(jnp.float32) + gate_up_other.astype(jnp.float32)).astype(
        jnp.bfloat16
    )
    ff_half = gate_up.shape[2] // 2
    gate_up_orders = (fsdp_order + ctx_order, ctx_order + fsdp_order)
    gate_up_open = [
        reduce_open(gate_up[:, :, index * ff_half : (index + 1) * ff_half], order)
        for index, order in enumerate(gate_up_orders)
    ]
    grad_resid, grad_ffn_gain_term = norm_back(part, residual, inverse_two, gain_ffn)
    grad_resid = grad_resid + grad_z.astype(jnp.float32)
    grad_attn_low = grad_resid.astype(jnp.bfloat16)
    out_product = by_owner(mixed_low, grad_attn_low)
    grad_mixed = grouped(contract_cols(grad_attn_low, out_full).astype(jnp.bfloat16))
    grad_queries, grad_keys, grad_values = attend_backward(
        queries,
        keys,
        values,
        query_pos,
        key_pos,
        lse,
        mixed_full,
        grad_mixed,
        gate_up_open[0][1],
        down_open[1],
    )
    grad_query_rot = ungrouped(grad_queries)
    grad_query_low = (
        unrotate(grad_query_rot, cosine_table, sine_table)
        .astype(jnp.bfloat16)
        .reshape(local_rows, HEADS * HEAD)
    )
    held = jnp.moveaxis(jnp.concatenate([grad_keys, grad_values], axis=0), 0, 1).reshape(
        pair_total, local_rows, 2 * kv_size
    )
    for bit in range(ctx_bits):
        pairs = held.reshape((held.shape[0] // 2, 2) + held.shape[1:])
        kept = pairs[:, 0].astype(jnp.float32) + swap(pairs[:, 1], "ctx", bit).astype(jnp.float32)
        held = kept.astype(jnp.bfloat16) if bit < ctx_bits - 1 else kept
    key_sum = held[0][:, :kv_size]
    value_sum = held[0][:, kv_size:]
    down_held, down_trail = reduce_owner(down_open, fsdp_order + ctx_order, key_sum)
    grad_down = spread_owner(down_held, [(0, down_dim)] + down_trail)[0].astype(jnp.float32)
    gate_up_sums = []
    for opened, part_order in zip(gate_up_open, gate_up_orders):
        gate_up_held, gate_up_trail = reduce_owner(opened, part_order, key_sum)
        gate_up_sums.append(spread_owner(gate_up_held, gate_up_trail)[0])
    gate_up_sum = jnp.concatenate(gate_up_sums, axis=1)
    gate_up_peer = swap(gate_up_sum, "ctx", 0)
    grad_w_gate = jnp.where(core == 0, gate_up_sum, gate_up_peer).astype(jnp.float32)
    grad_w_up = jnp.where(core == 0, gate_up_peer, gate_up_sum).astype(jnp.float32)
    full_order = core_order + fsdp_order + ctx_order
    out_held, out_trail = reduce_owner(
        reduce_open(tie(out_product, key_sum), full_order), full_order
    )
    grad_w_out = spread_owner(out_held, out_trail)[0].astype(jnp.float32)
    grad_key_low = (
        unrotate(key_sum.reshape(local_rows, KV_HEADS, HEAD), cosine_table, sine_table)
        .astype(jnp.bfloat16)
        .reshape(local_rows, KV_HEADS * HEAD)
    )
    grad_value_low = value_sum.astype(jnp.bfloat16)
    grad_qkv_low = jnp.concatenate([grad_query_low, grad_key_low, grad_value_low], axis=1)
    grad_normed_one = contract_cols(grad_qkv_low, qkv_full)
    grad_inputs, grad_attn_gain_term = norm_back(grad_normed_one, inputs, inverse_one, gain_attn)
    grad_in = (grad_resid + grad_inputs)[None]
    rows_owned = attn_gain.shape[0]
    gain_terms = jnp.stack([grad_attn_gain_term, grad_ffn_gain_term], axis=1).astype(jnp.bfloat16)
    qkv_product = by_owner(normed_one, grad_qkv_low)
    padding = -(qkv_size + 2) % 256
    qkv_parts = jnp.concatenate(
        [
            qkv_product,
            gain_terms.reshape(owners, rows_owned, 2),
            jnp.zeros((owners, rows_owned, padding), jnp.bfloat16),
        ],
        axis=2,
    )
    qkv_held, qkv_trail = reduce_owner(reduce_open(qkv_parts, full_order), full_order)
    qkv_sum = spread_owner(qkv_held, qkv_trail)[0].astype(jnp.float32)
    return (
        block_out,
        grad_in,
        qkv_sum[:, qkv_size],
        qkv_sum[:, :q_size],
        qkv_sum[:, q_size : q_size + kv_size],
        qkv_sum[:, q_size + kv_size : qkv_size],
        grad_w_out,
        qkv_sum[:, qkv_size + 1],
        grad_w_gate,
        grad_w_up,
        grad_down,
    )


def solution(mesh):
    placed = (
        P("fsdp", "ctx", None),
        P("fsdp", None),
        P("fsdp"),
        P("fsdp", None),
        P("fsdp", None),
        P("fsdp", None),
        P("fsdp", None),
        P("fsdp"),
        P("fsdp", None),
        P("fsdp", None),
        P("fsdp", None),
        P("fsdp", "ctx", None),
    )
    return jax.shard_map(
        body,
        mesh=mesh,
        in_specs=placed,
        out_specs=(
            P("fsdp", "ctx", None),
            P("fsdp", "ctx", None),
            P("fsdp"),
            P("fsdp", None),
            P("fsdp", None),
            P("fsdp", None),
            P("fsdp", None),
            P("fsdp"),
            P("fsdp", None),
            P("fsdp", None),
            P("fsdp", None),
        ),
        check_vma=False,
    )
```
